256 devices in a mesh: sample: 64 (over x, z, core), tensor: 4 (over y).
Axes of the slice: x: 4, y: 4, z: 8, core: 2. Of those that a mesh axis runs over, the one named last changes fastest.
Arguments:
- queries: bfloat16 [64, 256, 8192], P('sample', None, 'tensor'), may hold values from -48 to 48
- resp_keys: bfloat16 [64, 256, 1024], P('sample', None, 'tensor'), may hold values from -6 to 6
- resp_values: bfloat16 [64, 256, 1024], P('sample', None, 'tensor'), may hold values from -6 to 6
- prompt_keys: bfloat16 [64, 1024, 1024], P('sample', 'tensor'), may hold values from -8 to 8
- prompt_values: bfloat16 [64, 1024, 1024], P('sample', 'tensor'), may hold values from -6 to 6
- out_grad: bfloat16 [64, 256, 8192], P('sample', None, 'tensor'), may hold values from -48 to 48
- lengths: int32 [64], P('sample'), may hold values from 64 to 256, as said below
- owner: int32 [1], replicated, may hold values from 0 to 63
Outputs:
- grad_queries: bfloat16 [64, 256, 8192], P('sample', None, 'tensor')
- grad_resp_keys: bfloat16 [64, 256, 1024], P('sample', None, 'tensor')
- grad_resp_values: bfloat16 [64, 256, 1024], P('sample', None, 'tensor')
- grad_prompt_keys: float32 [1024, 1024], P('sample', 'tensor')
- grad_prompt_values: float32 [1024, 1024], P('sample', 'tensor')
The draws below stay inside these ranges and needn't reach their ends.
Inputs may be any that keep to these rules, and one draw needn't show every extreme that they name: `lengths`: some response has all 256 tokens live.
All inputs are finite; a program needn't handle non-finite values.
Results may differ from the reference program's by a relative error of at most 0.012.
The reference program's roundings to bfloat16 on the way (of `masked_grad`, `probs_half` and `scores_half`) count: a program that leaves them out, or rounds other values in their place, can miss the bound.
Values may be sent and summed in bfloat16 or wider, within the bound.
No kernel may reach another device: no remote copies, remote signals or barrier semaphores. Data moves between devices by JAX's collectives and lax.ppermute only.
A program may use at most 128 MiB of HBM per device.

```python
import jax
import jax.numpy as jnp
from jax import lax

QH = 64
KVH = 8
HD = 128
R = 256
P_SIZE = 1024
GROUP = 8
SAMPLES = 64


def draw_queries(key, part):
    key = jax.random.fold_in(key, 11)
    drawn = jax.random.truncated_normal(key, -6.0, 6.0, (SAMPLES, R, QH * HD), jnp.float32)
    return drawn.astype(jnp.bfloat16)


def draw_prompt_keys(key, part):
    key = jax.random.fold_in(key, 13)
    drawn = jax.random.truncated_normal(key, -6.0, 6.0, (SAMPLES, P_SIZE, KVH * HD), jnp.float32)
    return drawn.astype(jnp.bfloat16)


def draw_lengths(key, part):
    key = jax.random.fold_in(key, 23)
    drawn = jax.random.randint(key, (SAMPLES,), R // 4, R + 1, jnp.int32)
    longest = jax.random.randint(jax.random.fold_in(key, 5), (), 0, SAMPLES, jnp.int32)
    return drawn.at[longest].set(R)


def steps_of(rng, dims, cuts, smallest, largest):
    factor_of, own = 1.0, jax.random.fold_in(rng, 6)
    for position, blocks in cuts:
        heights = jnp.exp(jax.random.uniform(jax.random.fold_in(own, position), (blocks,), jnp.float32, smallest / len(cuts), largest / len(cuts)))
        factor_of = factor_of * jnp.repeat(heights, dims[position] // blocks).reshape([-1 if axis == position else 1 for axis in range(len(dims))])
    return factor_of


def centred(own_key, extent, spread, most, shards=(), kind=jnp.bfloat16):
    result = spread * jax.random.normal(own_key, extent, jnp.float32)
    if shards:
        result = result * steps_of(own_key, extent, shards, -0.22, 0.18)
    return jnp.clip(result, -most, most).astype(kind)


def setup_inputs(seed: int = 0) -> dict:
    seeds = jax.random.split(jax.random.key(seed), 9)
    queries = draw_queries(jax.random.fold_in(seeds[8], 71), 0)
    resp_keys = centred(seeds[1], (SAMPLES, R, KVH * HD), 1.0, 6.0, ((0, 64), (2, 4)))
    resp_values = centred(seeds[2], (SAMPLES, R, KVH * HD), 1.0, 6.0, ((0, 64), (2, 4)))
    prompt_keys = draw_prompt_keys(jax.random.fold_in(seeds[8], 71), 0)
    prompt_values = centred(seeds[4], (SAMPLES, P_SIZE, KVH * HD), 1.0, 6.0, ((0, 64), (1, 4)))
    out_grad = centred(seeds[5], (SAMPLES, R, QH * HD), 8.0, 48.0, ((0, 64), (2, 4)))
    lengths = draw_lengths(jax.random.fold_in(seeds[8], 71), 0)
    owner = jax.random.randint(seeds[7], (1,), 0, SAMPLES).astype(jnp.int32)
    return {"queries": queries, "resp_keys": resp_keys, "resp_values": resp_values, "prompt_keys": prompt_keys, "prompt_values": prompt_values, "out_grad": out_grad, "lengths": lengths, "owner": owner}


masked_score = -1.0e30


def sample_backward(query_rows, resp_key, resp_value, grad_rows, length_one, prompt_key, prompt_value):
    factor = 1.0 / (HD ** 0.5)
    query_heads = query_rows.astype(jnp.float32).reshape(R, KVH, GROUP, HD)
    all_keys = jnp.concatenate([prompt_key, resp_key], 0).astype(jnp.float32).reshape(P_SIZE + R, KVH, HD)
    all_values = jnp.concatenate([prompt_value, resp_value], 0).astype(jnp.float32).reshape(P_SIZE + R, KVH, HD)
    row_index = jnp.arange(R, dtype=jnp.int32)
    valid_rows = row_index < length_one
    masked_grad = jnp.where(valid_rows[:, None], grad_rows, jnp.zeros_like(grad_rows))
    grad_heads = masked_grad.astype(jnp.float32).reshape(R, KVH, GROUP, HD)
    col_index = jnp.arange(P_SIZE + R, dtype=jnp.int32)[None, :]
    own_index = col_index - P_SIZE
    allowed = (col_index < P_SIZE) | ((own_index <= row_index[:, None]) & (own_index < length_one))
    scores = jnp.einsum("rkgd,ckd->kgrc", query_heads, all_keys) * factor
    scores = jnp.where(allowed, scores, masked_score)
    top_score = jnp.max(scores, axis=-1, keepdims=True)
    weights = jnp.exp(scores - top_score)
    totals = jnp.sum(weights, axis=-1, keepdims=True)
    attn_probs = weights / totals
    probs_half = lax.optimization_barrier(attn_probs.astype(jnp.bfloat16)).astype(jnp.float32)
    attended = jnp.einsum("kgrc,ckd->rkgd", probs_half, all_values)
    row_dots = jnp.sum(grad_heads * attended, axis=-1).transpose(1, 2, 0)
    grad_probs = jnp.einsum("rkgd,ckd->kgrc", grad_heads, all_values)
    grad_scores = attn_probs * (grad_probs - row_dots[..., None])
    scores_half = lax.optimization_barrier(grad_scores.astype(jnp.bfloat16)).astype(jnp.float32)
    grad_query = jnp.einsum("kgrc,ckd->rkgd", scores_half, all_keys) * factor
    grad_key = jnp.einsum("kgrc,rkgd->ckd", scores_half, query_heads).reshape(P_SIZE + R, KVH * HD) * factor
    grad_value = jnp.einsum("kgrc,rkgd->ckd", probs_half, grad_heads).reshape(P_SIZE + R, KVH * HD)
    return (grad_query.reshape(R, QH * HD).astype(jnp.bfloat16),
            grad_key[P_SIZE:].astype(jnp.bfloat16),
            grad_value[P_SIZE:].astype(jnp.bfloat16),
            grad_key[:P_SIZE],
            grad_value[:P_SIZE])


def reference(queries, resp_keys, resp_values, prompt_keys, prompt_values, out_grad, lengths, owner):
    prompt_key = lax.dynamic_index_in_dim(prompt_keys, owner[0].astype(jnp.int32), 0, keepdims=False)
    prompt_value = lax.dynamic_index_in_dim(prompt_values, owner[0].astype(jnp.int32), 0, keepdims=False)

    def advance(running, sample_items):
        query_rows, resp_key, resp_value, grad_rows, length_one = sample_items
        grad_query, key_own, value_own, key_prompt, value_prompt = sample_backward(
            query_rows, resp_key, resp_value, grad_rows, length_one, prompt_key, prompt_value)
        return (running[0] + key_prompt, running[1] + value_prompt), (grad_query, key_own, value_own)

    initial = (jnp.zeros((P_SIZE, KVH * HD), jnp.float32), jnp.zeros((P_SIZE, KVH * HD), jnp.float32))
    prompt_sums, stacked = lax.scan(advance, initial, (queries, resp_keys, resp_values, out_grad, lengths))
    return stacked[0], stacked[1], stacked[2], prompt_sums[0], prompt_sums[1]
```

```python
import math

import jax
import jax.numpy as jnp
from jax import lax
from jax.experimental import pallas as pl
from jax.experimental.pallas import tpu as pltpu
from jax.sharding import Mesh
from jax.sharding import PartitionSpec as P

HD = 128
GROUP = 8
HEADS_PER_STEP = 4
X, Z, CORES = 4, 8, 2
CHIPS = X * Z
FACTOR = 1.0 / math.sqrt(HD)
TO_EXP2 = FACTOR * math.log2(math.e)
masked_score = -1e30
f32, bf16 = jnp.float32, jnp.bfloat16
CHIP_AXES = ("x", "z")
SWAP = [(0, 1), (1, 0)]


def dot(a, b, over=((1,), (0,))):
    return lax.dot_general(a, b, (over, ((), ())), preferred_element_type=f32)


def attention_kernel(
    flags, q_ref, g_ref, mine_ref, other_ref, ko_ref, vo_ref, *rest
):
    dq_ref, dko_ref, dvo_ref, keep_ref, send_ref = rest[-11:-6]
    k_all, v_all, k_turned, acc_k, acc_v, _ = rest[-6:]
    step, last = pl.program_id(0), pl.num_programs(0) - 1
    length, core = flags[0], flags[1]
    prompt, own, rows = mine_ref.shape[0], ko_ref.shape[0], q_ref.shape[0]

    @pl.when(step == 0)
    def _():
        @pl.when(core == 0)
        def _():
            k_all[:prompt] = mine_ref[...]
            v_all[:prompt] = other_ref[...]

        @pl.when(core != 0)
        def _():
            k_all[:prompt] = other_ref[...]
            v_all[:prompt] = mine_ref[...]

        k_all[prompt:] = ko_ref[...]
        v_all[prompt:] = vo_ref[...]
        k_turned[...] = k_all[...].T
        acc_k[...] = jnp.zeros_like(acc_k)
        acc_v[...] = jnp.zeros_like(acc_v)

    live = lax.broadcasted_iota(jnp.int32, (rows, 1), 0) < length
    key = lax.broadcasted_iota(jnp.int32, (own, rows), 0)
    row = lax.broadcasted_iota(jnp.int32, (own, rows), 1)
    allowed = (key <= row) & (key < length)
    turned = ((1,), (1,))
    for head in range(HEADS_PER_STEP):
        cols = slice(head * HD, (head + 1) * HD)
        q = q_ref[:, cols]
        g = jnp.where(live, g_ref[:, cols], 0).astype(bf16)
        s_p = dot(k_all[:prompt], q, turned)
        s_o = jnp.where(allowed, dot(k_all[prompt:], q, turned), masked_score)
        top = jnp.maximum(
            jnp.max(s_p, 0, keepdims=True), jnp.max(s_o, 0, keepdims=True)
        )
        e_p = jnp.exp2((s_p - top) * TO_EXP2)
        e_o = jnp.exp2((s_o - top) * TO_EXP2)
        total = jnp.sum(e_p, 0, keepdims=True) + jnp.sum(e_o, 0, keepdims=True)
        inverse = 1.0 / total
        p_p, p_o = e_p * inverse, e_o * inverse
        h_p, h_o = p_p.astype(bf16), p_o.astype(bf16)
        g_p = dot(v_all[:prompt], g, turned)
        g_o = dot(v_all[prompt:], g, turned)
        row_dot = jnp.sum(h_p.astype(f32) * g_p, 0, keepdims=True) + jnp.sum(
            h_o.astype(f32) * g_o, 0, keepdims=True
        )
        d_p = (p_p * (g_p - row_dot)).astype(bf16)
        d_o = (p_o * (g_o - row_dot)).astype(bf16)
        acc_v[:prompt] += dot(h_p, g)
        acc_v[prompt:] += dot(h_o, g)
        acc_k[:prompt] += dot(d_p, q)
        acc_k[prompt:] += dot(d_o, q)
        dq = dot(k_turned[:, :prompt], d_p) + dot(k_turned[:, prompt:], d_o)
        dq_ref[:, cols] = (dq.T * FACTOR).astype(bf16)

    @pl.when(step == last)
    def _():
        acc_k[...] = acc_k[...] * FACTOR
        dko_ref[...] = acc_k[prompt:].astype(bf16)
        dvo_ref[...] = acc_v[prompt:].astype(bf16)
        for chip in range(CHIPS):
            for which, acc in enumerate((acc_k, acc_v)):
                for half in range(2):
                    start = ((chip % 8) * 4 + half) * 32 + (chip // 8) * 8
                    to = slice(half * 8, half * 8 + 8)
                    keep_at = pl.multiple_of(start + core * 64, 8)
                    send_at = pl.multiple_of(start + (1 - core) * 64, 8)
                    keep_ref[chip, which, to] = acc[pl.ds(keep_at, 8)]
                    rest[-1][which, to] = acc[pl.ds(send_at, 8)]
                send_ref[chip, which] = rest[-1][which].astype(bf16)


def attention(flags, q, g, mine, other, ko, vo, group, carried):
    rows, prompt, own = q.shape[0], mine.shape[0], ko.shape[0]
    steps = GROUP // HEADS_PER_STEP
    heads = pl.BlockSpec((rows, HEADS_PER_STEP * HD), lambda s, f: (0, group * steps + s))
    whole = pl.BlockSpec((prompt, HD), lambda s, f: (0, 0))
    part = pl.BlockSpec((own, HD), lambda s, f: (0, group))
    share = pl.BlockSpec((CHIPS, 2, 16, HD), lambda s, f: (0, 0, 0, 0))
    keys = prompt + own
    return pl.pallas_call(
        attention_kernel,
        grid_spec=pltpu.PrefetchScalarGridSpec(
            num_scalar_prefetch=1,
            grid=(steps,),
            in_specs=[heads, heads, whole, whole, part, part]
            + [pl.BlockSpec(memory_space=pl.ANY)] * len(carried),
            out_specs=[heads, part, part, share, share],
            scratch_shapes=[
                pltpu.VMEM((keys, HD), bf16),
                pltpu.VMEM((keys, HD), bf16),
                pltpu.VMEM((HD, keys), bf16),
                pltpu.VMEM((keys, HD), f32),
                pltpu.VMEM((keys, HD), f32),
                pltpu.VMEM((2, 16, HD), f32),
            ],
        ),
        out_shape=[
            jax.ShapeDtypeStruct(q.shape, bf16),
            jax.ShapeDtypeStruct(ko.shape, bf16),
            jax.ShapeDtypeStruct(vo.shape, bf16),
            jax.ShapeDtypeStruct((CHIPS, 2, 16, HD), f32),
            jax.ShapeDtypeStruct((CHIPS, 2, 16, HD), bf16),
        ],
        input_output_aliases={7 + i: i for i in range(len(carried))},
        compiler_params=pltpu.CompilerParams(vmem_limit_bytes=48 * 1024 * 1024),
        cost_estimate=pl.CostEstimate(
            flops=12 * GROUP * rows * keys * HD,
            bytes_accessed=4 * 1024 * 1024,
            transcendentals=GROUP * rows * keys,
        ),
        name=f"attention_{group}",
    )(flags, q, g, mine, other, ko, vo, *carried)


def per_device(
    queries, resp_keys, resp_values, prompt_keys, prompt_values, out_grad, lengths, owner
):
    core = lax.axis_index("core")
    owner_chip, owner_core = owner[0] // CORES, owner[0] % CORES
    groups = resp_keys.shape[2] // HD
    tensors = lax.axis_size("tensor")
    block = prompt_keys.shape[1]
    piece = block // CHIPS

    pk, pv = prompt_keys[0], prompt_values[0]
    got = lax.ppermute(jnp.where(core == 0, pv, pk), "core", SWAP)
    slot = jnp.where(core == owner_core, jnp.where(core == 0, pk, pv), got)
    slot = slot.reshape(CHIPS, piece, tensors, groups, HD)

    flags = jnp.stack([lengths[0], core.astype(jnp.int32)])
    rows = []
    for group in range(groups):
        out = slot[:, :, :, group].transpose(0, 2, 1, 3)
        out = out.reshape(CHIPS * tensors, piece, HD)
        arrived = lax.all_to_all(out, ("x", "z", "tensor"), 0, 0, tiled=True)
        picked = lax.dynamic_slice_in_dim(arrived, owner_chip * tensors, tensors, 0)
        picked = picked.reshape(1, tensors * piece, HD)
        out = jnp.broadcast_to(picked, (CHIPS, tensors * piece, HD))
        mine = lax.all_to_all(out, CHIP_AXES, 0, 0, tiled=True)
        mine = mine.reshape(CHIPS * tensors * piece, HD)
        rows.append((mine, lax.ppermute(mine, "core", SWAP)))

    carried, sums = (), []
    for group in range(groups):
        mine, other = rows[group]
        *carried, keep, send = attention(
            flags, queries[0], out_grad[0], mine, other, resp_keys[0], resp_values[0], group, carried
        )
        pair = keep + lax.ppermute(send, "core", SWAP).astype(f32)
        shares = lax.all_to_all(pair.astype(bf16), CHIP_AXES, 0, 0, tiled=True)
        sums.append(jnp.sum(shares.astype(f32), axis=0))
    dq, dko, dvo = carried
    return (
        dq[None],
        dko[None],
        dvo[None],
        jnp.concatenate([s[0] for s in sums], axis=1),
        jnp.concatenate([s[1] for s in sums], axis=1),
    )


def solution(mesh):
    split = Mesh(
        mesh.devices.reshape(X, Z, CORES, mesh.shape["tensor"]),
        ("x", "z", "core", "tensor"),
    )
    sample = ("x", "z", "core")
    placed = (
        P(sample, None, "tensor"),
        P(sample, None, "tensor"),
        P(sample, None, "tensor"),
        P(sample, "tensor", None),
        P(sample, "tensor", None),
        P(sample, None, "tensor"),
        P(sample),
        P(),
    )
    return jax.shard_map(
        per_device,
        mesh=split,
        in_specs=placed,
        out_specs=(
            P(sample, None, "tensor"),
            P(sample, None, "tensor"),
            P(sample, None, "tensor"),
            P(sample, "tensor"),
            P(sample, "tensor"),
        ),
        check_vma=False,
    )
```
